32 devices in a mesh: row: 8 (over y, x, core), col: 4 (over z).
Axes of the slice: x: 2, y: 2, z: 4, core: 2. Of those that a mesh axis runs over, the one named last changes fastest.
Arguments:
- flow_state: float32 [6, 64, 64, 512], P(None, 'row', 'col'), may hold values from -6 to 6
- spectral: float32 [64, 64, 512], P('row', 'col'), may hold values from 0.5 to 2
- step_size: float32 [6], replicated, may hold values from 64 to 1024
- fringe_count: int32 [32, 32], P(('row', 'col')), may hold values from 0 to 32, as said below
- donor_base: int32 [32768], P(('row', 'col')), may hold values from 0 to 56830, as said below
- donor_frac: float32 [3, 32768], P(None, ('row', 'col')), may hold values from 0 to 1
- fringe_cell: int32 [32768], P(('row', 'col')), may hold values from 0 to 65535, as said below
Outputs:
- increment: float32 [6, 64, 64, 512], P(None, 'row', 'col')
The draws below stay inside these ranges and needn't reach their ends.
Inputs may be any that keep to these rules, and one draw needn't show every extreme that they name: `fringe_count`: entry [s, r] is how many fringe cells of device r take values from device s; for every device s, entry [s, (7 s + 3) mod 32] is 32 (so each sender fills all 32 slots of at least one receiver, and each receiver gets 32 from at least one sender); every other entry is 0 or between 16 and 32. `donor_base`: each value is the flat index of a cell whose j, k, l local indices are below 7, 15, 511. `fringe_cell`: the 1024 entries that belong to one receiving device are distinct cells of its block.
All inputs are finite; a program needn't handle non-finite values.
Results may differ from the reference program's by a relative error of at most 0.0003.
Values sent between devices are 32-bit elements; how exact they have to be, the bound alone decides.
A program may use at most 128 MiB of HBM per device.

```python
import math
import jax
import jax.numpy as jnp
from jax import lax

NV = 6
CJ = 8
CK = 16
CL = 512
CAP = 32
PEERS = 32
SLOTS = 1024
CELLS = 65536
NJ = 64
NK = 64
N_ROW = 8
N_COL = 4


def draw_fringe_count(key, part):
    first, second, third = jax.random.split(key, 3)
    level = jax.random.randint(first, (PEERS, 1), 0, 8)
    active = jax.random.randint(second, (PEERS, PEERS), 0, 8) <= level
    counts = jax.random.randint(third, (PEERS, PEERS), CAP // 2, CAP + 1)
    counts = jnp.where(active, counts, 0)
    senders = lax.broadcasted_iota(jnp.int32, (PEERS, PEERS), 0)
    receivers = lax.broadcasted_iota(jnp.int32, (PEERS, PEERS), 1)
    full = receivers == (7 * senders + 3) % PEERS
    return jnp.where(full, CAP, counts).astype(jnp.int32)


def draw_donor_base(key, part):
    first, second, third = jax.random.split(jax.random.fold_in(key, 11), 3)
    total = PEERS * SLOTS
    index_j = jax.random.randint(first, (total,), 0, CJ - 1)
    index_k = jax.random.randint(second, (total,), 0, CK - 1)
    index_l = jax.random.randint(third, (total,), 0, CL - 1)
    base = index_j * (CK * CL) + index_k * CL + index_l
    position = jnp.arange(total, dtype=jnp.int32) % SLOTS
    highest = (CJ - 2) * CK * CL + (CK - 2) * CL + CL - 2
    base = jnp.where(position == 0, highest, jnp.where(position == 1, 0, base))
    return base.astype(jnp.int32)


def draw_fringe_cell(key, part):
    device_keys = jax.random.split(jax.random.fold_in(key, 23), PEERS)

    def one_device(device_key):
        first, second = jax.random.split(device_key)
        inner = jax.random.permutation(first, CELLS - 2) + 1
        picked = jnp.concatenate([jnp.array([0, CELLS - 1], jnp.int32), inner[:SLOTS - 2].astype(jnp.int32)])
        order = jax.random.permutation(second, SLOTS)
        return picked[order]
    return jax.vmap(one_device)(device_keys).reshape(-1).astype(jnp.int32)


def shard_levels(key, dims, cuts, smallest, largest):
    factor_of, own = 1.0, jax.random.fold_in(key, 6)
    for dim, shards_of in cuts:
        steps = jnp.exp(jax.random.uniform(jax.random.fold_in(own, dim), (shards_of,), jnp.float32, smallest / len(cuts), largest / len(cuts)))
        factor_of = factor_of * jnp.repeat(steps, dims[dim] // shards_of).reshape([-1 if axis == dim else 1 for axis in range(len(dims))])
    return factor_of


def noise(stream_key, dims, spread, reach, cuts=(), kind=jnp.bfloat16):
    values = spread * jax.random.normal(stream_key, dims, jnp.float32)
    if cuts:
        values = values * shard_levels(stream_key, dims, cuts, -0.22, 0.18)
    return jnp.clip(values, -reach, reach).astype(kind)


def setup_inputs(seed: int = 0) -> dict:
    splits = jax.random.split(jax.random.key(seed), 8)
    return {
        "flow_state": noise(splits[0], (NV, NJ, NK, CL), 1.0, 6.0, ((1, 8), (2, 4)), jnp.float32),
        "spectral": jnp.clip(jnp.exp(math.log(2.0) - 1.3862944 * jax.random.uniform(splits[1], (NJ, NK, CL), jnp.float32) ** shard_levels(splits[1], (NJ, NK, CL), ((0, 8), (1, 4)), -0.2, 0.2)), 0.5, 2.0),
        "step_size": jnp.clip(jnp.exp(jax.random.uniform(splits[2], (NV,), jnp.float32, math.log(64.0), math.log(1024.0))), 64.0, 1024.0),
        "fringe_count": draw_fringe_count(jax.random.fold_in(splits[7], 71), 0),
        "donor_base": draw_donor_base(jax.random.fold_in(splits[7], 71), 0),
        "donor_frac": jnp.clip(1.0 * jax.random.uniform(splits[5], (3, PEERS * SLOTS), jnp.float32) ** shard_levels(splits[5], (3, PEERS * SLOTS), ((1, 32),), -0.2, 0.2), 0.0, 1.0),
        "fringe_cell": draw_fringe_cell(jax.random.fold_in(splits[7], 71), 0),
    }


def implicit_factor(length, step_rates):
    position = jnp.arange(length)
    second = (jnp.where(position[:, None] == position[None, :], -2.0, 0.0) + jnp.where(jnp.abs(position[:, None] - position[None, :]) == 1, 1.0, 0.0)).astype(jnp.float32)
    fourth = jnp.dot(second, second, precision=lax.Precision.HIGHEST)
    operator_matrix = -second + 0.25 * fourth
    identity = jnp.eye(length, dtype=jnp.float32)
    return jax.vmap(lambda one_rate: jnp.linalg.cholesky(identity + one_rate * operator_matrix))(step_rates)

def solve_lines(factors, columns):
    return jax.vmap(lambda factor_one, right_side: jax.scipy.linalg.cho_solve((factor_one, True), right_side))(factors, columns)

def interpolate(flat_block, base_index, fraction, k_cells, l_cells):
    total = jnp.zeros((flat_block.shape[0], base_index.shape[0]), jnp.float32)
    for shift_j in (0, 1):
        for shift_k in (0, 1):
            for shift_l in (0, 1):
                weight_j = fraction[0] if shift_j else 1.0 - fraction[0]
                weight_k = fraction[1] if shift_k else 1.0 - fraction[1]
                weight_l = fraction[2] if shift_l else 1.0 - fraction[2]
                weight = weight_j * weight_k * weight_l
                picked = flat_block[:, base_index + shift_j * k_cells * l_cells + shift_k * l_cells + shift_l]
                total = total + weight[None, :] * picked
    return total

def place_fringe(block_one, arrived_one, alive_one, target_one):
    current = block_one[:, target_one]
    return block_one.at[:, target_one].set(jnp.where(alive_one[None, :], arrived_one, current))

def reference(flow_state, spectral, step_size, fringe_count, donor_base, donor_frac, fringe_cell):
    devices_all = N_ROW * N_COL
    blocks = flow_state.reshape(NV, N_ROW, CJ, N_COL, CK, CL).transpose(1, 3, 0, 2, 4, 5).reshape(devices_all, NV, CELLS)
    bases = donor_base.reshape(devices_all, SLOTS)
    fractions = donor_frac.reshape(3, devices_all, SLOTS).transpose(1, 0, 2)
    sent = jax.vmap(lambda block_one, base_one, frac_one: interpolate(block_one, base_one, frac_one, CK, CL))(blocks, bases, fractions)
    arrived = sent.reshape(devices_all, NV, devices_all, CAP).transpose(2, 1, 0, 3).reshape(devices_all, NV, SLOTS)
    counts = jnp.repeat(fringe_count.T, CAP, axis=1)
    position = jnp.arange(SLOTS, dtype=jnp.int32) % CAP
    alive = position[None, :] < counts
    targets = fringe_cell.reshape(devices_all, SLOTS)
    blocks = jax.vmap(place_fringe)(blocks, arrived, alive, targets)
    filled = blocks.reshape(N_ROW, N_COL, NV, CJ, CK, CL).transpose(2, 0, 3, 1, 4, 5).reshape(NV, NJ, NK, CL)
    padded = jnp.pad(filled, ((0, 0), (1, 1), (1, 1), (1, 1)))
    center = padded[:, 1:-1, 1:-1, 1:-1]
    laplace = padded[:, 2:, 1:-1, 1:-1] + padded[:, :-2, 1:-1, 1:-1] + padded[:, 1:-1, 2:, 1:-1] + padded[:, 1:-1, :-2, 1:-1] + padded[:, 1:-1, 1:-1, 2:] + padded[:, 1:-1, 1:-1, :-2] - 6.0 * center
    update = step_size[:, None, None, None] * (spectral[None] * laplace)
    factors_l = implicit_factor(CL, step_size)
    factors_j = implicit_factor(NJ, step_size)
    factors_k = implicit_factor(NK, step_size)
    along_l = solve_lines(factors_l, update.reshape(NV, NJ * NK, CL).transpose(0, 2, 1)).transpose(0, 2, 1).reshape(NV, NJ, NK, CL)
    along_j = solve_lines(factors_j, along_l.reshape(NV, NJ, NK * CL)).reshape(NV, NJ, NK, CL)
    moved = along_j.transpose(0, 2, 1, 3).reshape(NV, NK, NJ * CL)
    along_k = solve_lines(factors_k, moved).reshape(NV, NK, NJ, CL).transpose(0, 2, 1, 3)
    return along_k
```

```python
import functools

import jax
import jax.numpy as jnp
import ml_dtypes
import numpy as np
from jax import lax
from jax.experimental import pallas as pl
from jax.experimental.pallas import tpu as pltpu
from jax.sharding import PartitionSpec as P

F32 = jnp.float32
BF16 = jnp.bfloat16
MESH = pl.DeviceIdType.MESH
CHUNK = 1024


def dot(a, b):
    return jnp.dot(a, b, precision=lax.Precision.HIGHEST, preferred_element_type=F32)


def split(a):
    high = a.astype(BF16)
    return high, (a - high.astype(F32)).astype(BF16)


def dot_split(a, b_high, b_low):
    a_high, a_low = split(a)
    single = functools.partial(jnp.dot, preferred_element_type=F32)
    return single(a_high, b_high) + single(a_low, b_high) + single(a_high, b_low)


def iota(shape, dim):
    return lax.broadcasted_iota(jnp.int32, shape, dim)


def decay(distance, theta):
    return jnp.exp(-distance * theta)


def line_matrices(par, v, scales, position, block, total, local_of, other_of, others):
    rows = block * others
    theta = (par[v, 0], par[v, 1])
    first = (position * block).astype(F32)
    n1 = float(total + 1)
    r, q = iota((rows, rows), 0), iota((rows, rows), 1)
    i = first + local_of(r).astype(F32) + 1.0
    j = first + local_of(q).astype(F32) + 1.0
    low, high = jnp.minimum(i, j), jnp.maximum(i, j)
    own = jnp.zeros((rows, rows), F32)
    for m in (0, 1):
        own = own + scales[m] * decay(high - low, theta[m]) * (1.0 - decay(2.0 * low, theta[m])) * (
            1.0 - decay(2.0 * (n1 - high), theta[m])
        )
    own = jnp.where(other_of(r) == other_of(q), own, 0.0)

    def side_mode_other(t):
        side = t >= 2 * others
        within = jnp.where(side, t - 2 * others, t)
        mode = within >= others
        return side, mode, jnp.where(mode, within - others, within)

    r, q = iota((4 * others, rows), 0), iota((4 * others, rows), 1)
    side, mode, other = side_mode_other(r)
    angle = jnp.where(mode, theta[1], theta[0])
    j = local_of(q).astype(F32) + 1.0
    distance = jnp.where(side, j, block + 1.0 - j)
    edge = jnp.where(side, n1 - first - j, first + j)
    outgoing = decay(distance, angle) * (1.0 - decay(2.0 * edge, angle))
    outgoing = jnp.where(other == other_of(q), outgoing, 0.0)

    r, q = iota((rows, 4 * others), 0), iota((rows, 4 * others), 1)
    side, mode, other = side_mode_other(q)
    angle = jnp.where(mode, theta[1], theta[0])
    i = local_of(r).astype(F32) + 1.0
    distance = jnp.where(side, block - i, i - 1.0)
    edge = jnp.where(side, first + i, n1 - first - i)
    incoming = decay(distance, angle) * (1.0 - decay(2.0 * edge, angle)) * jnp.where(mode, scales[1], scales[0])
    incoming = jnp.where(other == other_of(r), incoming, 0.0)
    return own, outgoing, incoming


def kernel(
    nrow, ncol, bj, bk,
    x_ref, spec_ref, par, base_ref, frac_ref, alive_ref, cell_ref, shape_ref, sh_ref, sl_ref,
    out_ref,
    sent_ref, arr_ref, val_ref, fill_ref, upd_ref, mask_ref,
    hj_lo, hj_hi, hk_lo, hk_hi, ks_lo, ks_hi,
    gj, wj, uj, gk, wk, uk,
    own_j, in_j, snd_j, own_k, in_k, snd_k,
    f_send, f_recv, h_send, h_recv, j_send, j_recv, k_send, k_recv,
):
    nv, rows, bl = x_ref.shape
    ndev = nrow * ncol
    r, c = lax.axis_index("row"), lax.axis_index("col")
    me = r * ncol + c
    slots = base_ref.shape[1]
    cap = slots // ndev
    shift_k = bk.bit_length() - 1
    shift_l = bl.bit_length() - 1

    barrier = pltpu.get_barrier_semaphore()

    @pl.loop(1, ndev)
    def _(d):
        p = lax.rem(me + d, ndev)
        pl.semaphore_signal(barrier, inc=1, device_id=(p // ncol, lax.rem(p, ncol)), device_id_type=MESH)

    for t0 in range(0, slots, CHUNK):
        lanes = pl.ds(t0, CHUNK)
        base = base_ref[:, lanes]
        fj, fk, fl = frac_ref[0:1, lanes], frac_ref[1:2, lanes], frac_ref[2:3, lanes]
        cell_row = lax.shift_right_logical(base, shift_l)
        cell_l = base & (bl - 1)
        row = iota((rows, CHUNK), 0)
        weight = jnp.zeros((rows, CHUNK), F32)
        for a in (0, 1):
            for b in (0, 1):
                w = (fj if a else 1.0 - fj) * (fk if b else 1.0 - fk)
                weight = weight + jnp.where(row == cell_row + (a * bk + b), w, 0.0)
        w_high, w_low = split(weight)
        lane = iota((bl, CHUNK), 0)
        weight_l = jnp.where(lane == cell_l, 1.0 - fl, 0.0) + jnp.where(lane == cell_l + 1, fl, 0.0)
        for v in range(nv):
            x_high, x_low = split(x_ref[v].T)
            single = functools.partial(jnp.dot, preferred_element_type=F32)
            part = single(x_high, w_high) + single(x_low, w_high) + single(x_high, w_low)
            val_ref[v : v + 1, lanes] = jnp.sum(part * weight_l, axis=0, keepdims=True)
        val_ref[nv : nv + 1, lanes] = alive_ref[:, lanes]
    for p in range(ndev):
        sent_ref[p, :, 0:cap] = val_ref[:, p * cap : (p + 1) * cap]

    pl.semaphore_wait(barrier, ndev - 1)

    def fringe(p, q):
        return pltpu.make_async_remote_copy(
            src_ref=sent_ref.at[p], dst_ref=arr_ref.at[q], send_sem=f_send.at[p], recv_sem=f_recv.at[q],
            device_id=(p // ncol, lax.rem(p, ncol)), device_id_type=MESH,
        )

    @pl.loop(1, ndev)
    def _(d):
        fringe(lax.rem(me + d, ndev), me).start()

    arr_ref[me] = sent_ref[me]

    @pl.loop(0, nv)
    def _(v):
        own, outgoing, incoming = line_matrices(
            par, v, (par[v, 2], par[v, 3]), r, bj, bj * nrow,
            lambda t: lax.shift_right_logical(t, shift_k), lambda t: t & (bk - 1), bk,
        )
        gj[v], wj[v], uj[v] = own, outgoing, incoming
        own, outgoing, incoming = line_matrices(
            par, v, (par[v, 4], par[v, 5]), c, bk, bk * ncol,
            lambda t: t & (bk - 1), lambda t: lax.shift_right_logical(t, shift_k), bj,
        )
        gk[v], wk[v], uk[v] = own, outgoing, incoming

    @pl.loop(1, ndev)
    def _(d):
        p = lax.rem(me + ndev - d, ndev)
        fringe(p, p).wait_recv()

    for p in range(ndev):
        val_ref[:, p * cap : (p + 1) * cap] = arr_ref[p, :, 0:cap]

    mask_ref[...] = jnp.zeros_like(mask_ref)
    fill_ref[...] = jnp.zeros_like(fill_ref)
    contract = (((1,), (1,)), ((), ()))
    for t0 in range(0, slots, CHUNK):
        lanes = pl.ds(t0, CHUNK)
        cell = cell_ref[:, lanes]
        alive = val_ref[nv : nv + 1, lanes] > 0.5
        at_row = (iota((rows, CHUNK), 0) == lax.shift_right_logical(cell, shift_l)) & alive
        at_lane = jnp.where(iota((bl, CHUNK), 0) == (cell & (bl - 1)), 1.0, 0.0).astype(BF16)
        place = functools.partial(lax.dot_general, dimension_numbers=contract, preferred_element_type=F32)
        mask_ref[...] += place(jnp.where(at_row, 1.0, 0.0).astype(BF16), at_lane)
        for v in range(nv):
            value = jnp.where(at_row, val_ref[v : v + 1, lanes], 0.0)
            high, low = split(value)
            rest = (value - high.astype(F32) - low.astype(F32)).astype(BF16)
            fill_ref[v] += place(high, at_lane) + place(low, at_lane) + place(rest, at_lane)

    @pl.loop(0, nv)
    def _(v):
        filled = jnp.where(mask_ref[...] > 0.5, fill_ref[v], x_ref[v])
        fill_ref[v] = filled
        planes = filled.reshape(bj, bk, bl)
        ks_lo[v] = planes[:, bk - 1, :]
        ks_hi[v] = planes[:, 0, :]

    halos = (
        (r < nrow - 1, r > 0, fill_ref.at[:, pl.ds(rows - bk, bk)], hj_lo, (r + 1, c)),
        (r > 0, r < nrow - 1, fill_ref.at[:, pl.ds(0, bk)], hj_hi, (r - 1, c)),
        (c < ncol - 1, c > 0, ks_lo, hk_lo, (r, c + 1)),
        (c > 0, c < ncol - 1, ks_hi, hk_hi, (r, c - 1)),
    )

    def halo(h):
        _, _, source, target, device = halos[h]
        return pltpu.make_async_remote_copy(
            src_ref=source, dst_ref=target, send_sem=h_send.at[h], recv_sem=h_recv.at[h],
            device_id=device, device_id_type=MESH,
        )

    for h in range(4):
        pl.when(halos[h][0])(lambda h=h: halo(h).start())

        @pl.when(jnp.logical_not(halos[h][1]))
        def _(h=h):
            halos[h][3][...] = jnp.zeros_like(halos[h][3])

    for h in range(4):
        pl.when(halos[h][1])(lambda h=h: halo(h).wait_recv())

    lane = iota((rows, bl), 1)
    k_of = iota((rows, bl), 0) & (bk - 1)

    def spread(plane):
        return jnp.broadcast_to(plane[:, None, :], (bj, bk, bl)).reshape(rows, bl)

    @pl.loop(0, nv)
    def _(v):
        f = fill_ref[v]
        total = jnp.concatenate([f[bk:], hj_hi[v]], axis=0) + jnp.concatenate([hj_lo[v], f[:-bk]], axis=0)
        total = total + jnp.where(k_of == bk - 1, spread(hk_hi[v]), pltpu.roll(f, rows - 1, 0))
        total = total + jnp.where(k_of == 0, spread(hk_lo[v]), pltpu.roll(f, 1, 0))
        total = total + jnp.where(lane == bl - 1, 0.0, pltpu.roll(f, bl - 1, 1))
        total = total + jnp.where(lane == 0, 0.0, pltpu.roll(f, 1, 1))
        u = par[v, 6] * (spec_ref[...] * (total - 6.0 * f))
        upd_ref[v] = u
        own_j[v] = dot(wj[v], u)

    def chain(position, count, place_of, half, own, arrive, send, s_sem, r_sem, alpha):
        def hop(side, v):
            target = place_of(position + (1 if side == 0 else -1))
            return pltpu.make_async_remote_copy(
                src_ref=send.at[side, v], dst_ref=arrive.at[v, pl.ds(side * half, half)],
                send_sem=s_sem.at[side, v], recv_sem=r_sem.at[side, v], device_id=target, device_id_type=MESH,
            )

        has_in = (position > 0, position < count - 1)
        has_out = (position < count - 1, position > 0)

        def pass_on(side):
            @pl.when(jnp.logical_not(has_in[side]))
            def _():
                arrive[:, pl.ds(side * half, half), :] = jnp.zeros((nv, half, bl), F32)

            @pl.loop(0, nv)
            def _(v):
                pl.when(has_in[side])(lambda: hop(side, v).wait_recv())

                @pl.when(has_out[side])
                def _():
                    came = arrive[v, pl.ds(side * half, half), :]
                    factor = jnp.where(iota((half, bl), 0) < half // 2, par[v, alpha], par[v, alpha + 1])
                    send[side, v] = own[v, pl.ds(side * half, half), :] + factor * came
                    hop(side, v).start()

        @pl.when(position < count // 2)
        def _():
            pass_on(0)
            pass_on(1)

        @pl.when(position >= count // 2)
        def _():
            pass_on(1)
            pass_on(0)

        def finish():
            for side in (0, 1):

                @pl.when(has_out[side])
                def _(side=side):
                    @pl.loop(0, nv)
                    def _(v):
                        hop(side, v).wait_send()

        return finish

    finish_j = chain(r, nrow, lambda p: (p, c), 2 * bk, own_j, in_j, snd_j, j_send, j_recv, 7)

    @pl.loop(0, nv)
    def _(v):
        y = dot(gj[v], upd_ref[v]) + dot(uj[v], in_j[v])
        upd_ref[v] = y
        own_k[v] = dot(wk[v], y)

    finish_k = chain(c, ncol, lambda p: (r, p), 2 * bj, own_k, in_k, snd_k, k_send, k_recv, 9)

    @pl.loop(0, nv)
    def _(v):
        y = dot(gk[v], upd_ref[v]) + dot(uk[v], in_k[v])
        wave = dot_split(y, sh_ref[...], sl_ref[...])
        wave = wave / (par[v, 11] + par[v, 6] * shape_ref[...])
        out_ref[v] = dot_split(wave, sh_ref[...], sl_ref[...])

    finish_j()
    finish_k()
    for h in range(4):
        pl.when(halos[h][0])(lambda h=h: halo(h).wait_send())

    @pl.loop(1, ndev)
    def _(d):
        fringe(lax.rem(me + d, ndev), me).wait_send()


def parameters(step, bj, bk, nrow, ncol):
    product = 3.5 * step
    diagonal = 1.0 + product
    unit = (diagonal - product) - ((4.0 * step - product) - 0.5 * step)
    unit = unit / 1.0
    s = step / unit
    root = jnp.sqrt(1.0 - 1.0 / s)
    b = 2.0 + 2.0 * root
    a = 4.0 / (s * b)
    kappa = 1.0 / (s * root * unit)

    def angle(x):
        return 2.0 * jnp.arcsinh(0.5 * jnp.sqrt(x))

    def scale(x, theta, n):
        return kappa / (2.0 * jnp.sqrt(x + 0.25 * x * x) * (1.0 - jnp.exp(-2.0 * (n + 1) * theta)))

    ta, tb = angle(a), angle(b)
    nj, nk = bj * nrow, bk * ncol
    return jnp.stack(
        [
            ta, tb, scale(a, ta, nj), -scale(b, tb, nj), scale(a, ta, nk), -scale(b, tb, nk), step,
            jnp.exp(-bj * ta), jnp.exp(-bj * tb), jnp.exp(-bk * ta), jnp.exp(-bk * tb), unit,
        ],
        axis=1,
    )


def sine_constants(n):
    k = np.arange(1, n + 1)
    s = np.sqrt(2.0 / (n + 1)) * np.sin(np.pi * ((k[:, None] * k[None, :]) % (2 * (n + 1))) / (n + 1))
    high = s.astype(ml_dtypes.bfloat16)
    low = (s - high.astype(np.float64)).astype(ml_dtypes.bfloat16)
    lam = 4.0 * np.sin(np.pi * k / (2.0 * (n + 1))) ** 2
    return high, low, (lam + 0.25 * lam * lam).astype(np.float32)[None, :]


def local(nrow, ncol, flow_state, spectral, step_size, fringe_count, donor_base, donor_frac, fringe_cell):
    nv, bj, bk, bl = flow_state.shape
    rows = bj * bk
    ndev = nrow * ncol
    slots = donor_base.shape[0]
    cap = slots // ndev
    alive = (jnp.arange(cap, dtype=jnp.int32)[None, :] < fringe_count.reshape(ndev, 1)).astype(F32)
    high, low, shape = sine_constants(bl)
    vmem = pl.BlockSpec(memory_space=pltpu.VMEM)
    smem = pl.BlockSpec(memory_space=pltpu.SMEM)
    big = pltpu.VMEM((nv, rows, bl), F32)
    dma = pltpu.SemaphoreType.DMA
    out = pl.pallas_call(
        functools.partial(kernel, nrow, ncol, bj, bk),
        out_shape=jax.ShapeDtypeStruct((nv, rows, bl), F32),
        in_specs=[vmem, vmem, smem] + [vmem] * 7,
        out_specs=vmem,
        scratch_shapes=[
            pltpu.VMEM((ndev, 8, 128), F32),
            pltpu.VMEM((ndev, 8, 128), F32),
            pltpu.VMEM((8, slots), F32),
            big,
            big,
            pltpu.VMEM((rows, bl), F32),
            pltpu.VMEM((nv, bk, bl), F32),
            pltpu.VMEM((nv, bk, bl), F32),
            pltpu.VMEM((nv, bj, bl), F32),
            pltpu.VMEM((nv, bj, bl), F32),
            pltpu.VMEM((nv, bj, bl), F32),
            pltpu.VMEM((nv, bj, bl), F32),
            pltpu.VMEM((nv, rows, rows), F32),
            pltpu.VMEM((nv, 4 * bk, rows), F32),
            pltpu.VMEM((nv, rows, 4 * bk), F32),
            pltpu.VMEM((nv, rows, rows), F32),
            pltpu.VMEM((nv, 4 * bj, rows), F32),
            pltpu.VMEM((nv, rows, 4 * bj), F32),
            pltpu.VMEM((nv, 4 * bk, bl), F32),
            pltpu.VMEM((nv, 4 * bk, bl), F32),
            pltpu.VMEM((2, nv, 2 * bk, bl), F32),
            pltpu.VMEM((nv, 4 * bj, bl), F32),
            pltpu.VMEM((nv, 4 * bj, bl), F32),
            pltpu.VMEM((2, nv, 2 * bj, bl), F32),
            dma((ndev,)),
            dma((ndev,)),
            dma((4,)),
            dma((4,)),
            dma((2, nv)),
            dma((2, nv)),
            dma((2, nv)),
            dma((2, nv)),
        ],
        compiler_params=pltpu.CompilerParams(
            collective_id=0, has_side_effects=True, vmem_limit_bytes=56 * 1024 * 1024
        ),
    )(
        flow_state.reshape(nv, rows, bl),
        spectral.reshape(rows, bl),
        parameters(step_size, bj, bk, nrow, ncol),
        donor_base.reshape(1, slots),
        donor_frac,
        alive.reshape(1, slots),
        fringe_cell.reshape(1, slots),
        jnp.asarray(shape),
        jnp.asarray(high),
        jnp.asarray(low),
    )
    return out.reshape(nv, bj, bk, bl)


def solution(mesh):
    placed = (
        P(None, "row", "col", None),
        P("row", "col", None),
        P(),
        P(("row", "col"), None),
        P(("row", "col")),
        P(None, ("row", "col")),
        P(("row", "col")),
    )
    return jax.shard_map(
        functools.partial(local, mesh.shape["row"], mesh.shape["col"]),
        mesh=mesh, in_specs=placed, out_specs=P(None, "row", "col", None), check_vma=False,
    )
```

```python
import functools

import jax
import jax.numpy as jnp
import ml_dtypes
import numpy as np
from jax import lax
from jax.experimental import pallas as pl
from jax.experimental.pallas import tpu as pltpu
from jax.sharding import PartitionSpec as P

F32 = jnp.float32
BF16 = jnp.bfloat16
MESH = pl.DeviceIdType.MESH
CHUNK = 256


def split(a):
    high = a.astype(BF16)
    return high, (a - high.astype(F32)).astype(BF16)


def dot_split(a, b_high, b_low):
    a_high, a_low = split(a)
    single = functools.partial(jnp.dot, preferred_element_type=F32)
    return single(a_high, b_high) + single(a_low, b_high) + single(a_high, b_low)


def iota(shape, dim):
    return lax.broadcasted_iota(jnp.int32, shape, dim)


def decay(distance, theta):
    return jnp.exp(-distance * theta)


def dot3(a, b):
    b_high, b_low = split(b)
    return dot_split(a, b_high, b_low)


def line_matrices(theta, scales, position, block, total, local_of, other_of, others, expand):
    rows = block * others
    first = (position * block).astype(F32)
    n1 = float(total + 1)
    i = first + iota((block, rows), 0).astype(F32) + 1.0
    j = first + local_of(iota((block, rows), 1)).astype(F32) + 1.0
    low, high = jnp.minimum(i, j), jnp.maximum(i, j)
    own = jnp.zeros((block, rows), F32)
    for m in (0, 1):
        own = own + scales[m] * decay(high - low, theta[m]) * (1.0 - decay(2.0 * low, theta[m])) * (
            1.0 - decay(2.0 * (n1 - high), theta[m])
        )
    own = jnp.where(other_of(iota((rows, rows), 0)) == other_of(iota((rows, rows), 1)), expand(own), 0.0)

    j = local_of(iota((1, rows), 1)).astype(F32) + 1.0
    parts = []
    for side in (0, 1):
        for m in (0, 1):
            distance = j if side else block + 1.0 - j
            edge = n1 - first - j if side else first + j
            value = decay(distance, theta[m]) * (1.0 - decay(2.0 * edge, theta[m]))
            same = iota((others, rows), 0) == other_of(iota((others, rows), 1))
            parts.append(jnp.where(same, value, 0.0))
    outgoing = jnp.concatenate(parts, axis=0)

    width = 4 * others
    t = iota((block, width), 1)
    side = t >= 2 * others
    mode = jnp.where(side, t - 2 * others, t) >= others
    angle = jnp.where(mode, theta[1][:, :width], theta[0][:, :width])
    i = iota((block, width), 0).astype(F32) + 1.0
    distance = jnp.where(side, block - i, i - 1.0)
    edge = jnp.where(side, first + i, n1 - first - i)
    incoming = decay(distance, angle) * (1.0 - decay(2.0 * edge, angle))
    incoming = incoming * jnp.where(mode, scales[1][:, :width], scales[0][:, :width])
    other = iota((rows, width), 1) & (others - 1)
    incoming = jnp.where(other == other_of(iota((rows, width), 0)), expand(incoming), 0.0)
    return own, outgoing, incoming


def kernel(
    nrow, ncol, bj, bk,
    x_ref, spec_ref, step_ref, count_ref, base_ref, frac_ref, cell_ref, shape_ref, sh_ref, sl_ref,
    out_ref,
    sent_ref, arr_ref, val_ref, fill_ref, upd_ref, xh_ref, xl_ref, el_ref, lhs_ref, par_ref, inv_ref,
    hj_lo, hj_hi, hk_lo, hk_hi, ks_lo, ks_hi,
    gj, wj, uj, gk, wk, uk,
    own_j, in_j, snd_j, own_k, in_k, snd_k,
    f_send, f_recv, h_send, h_recv, j_send, j_recv, k_send, k_recv,
):
    nv, rows, bl = x_ref.shape
    ndev = nrow * ncol
    r, c = lax.axis_index("row"), lax.axis_index("col")
    me = r * ncol + c
    slots = base_ref.shape[1]
    cap = slots // ndev
    shift_k = bk.bit_length() - 1
    shift_l = bl.bit_length() - 1
    half_v = nv // 2
    single = functools.partial(jnp.dot, preferred_element_type=F32)

    barrier = pltpu.get_barrier_semaphore()

    @pl.loop(1, ndev)
    def _(d):
        p = lax.rem(me + d, ndev)
        pl.semaphore_signal(barrier, inc=1, device_id=(p // ncol, lax.rem(p, ncol)), device_id_type=MESH)

    @pl.loop(0, nv)
    def _(v):
        here = pl.ds(pl.multiple_of(v * rows, rows), rows)
        xh_ref[here, :], xl_ref[here, :] = split(x_ref[v])

    @pl.loop(0, slots // CHUNK)
    def _(t):
        lanes = pl.ds(pl.multiple_of(t * CHUNK, CHUNK), CHUNK)
        base = base_ref[:, lanes]
        fj, fk, fl = frac_ref[0:1, lanes], frac_ref[1:2, lanes], frac_ref[2:3, lanes]
        cell_row = lax.shift_right_logical(base, shift_l)
        cell_l = base & (bl - 1)
        row = iota((rows, CHUNK), 0)
        weight = jnp.zeros((rows, CHUNK), F32)
        for a in (0, 1):
            for b in (0, 1):
                w = (fj if a else 1.0 - fj) * (fk if b else 1.0 - fk)
                weight = jnp.where(row == cell_row + (a * bk + b), w, weight)
        lane = iota((bl, CHUNK), 0)
        weight_l = jnp.where(lane == cell_l, 1.0 - fl, jnp.where(lane == cell_l + 1, fl, 0.0))
        w_high, w_low = split(weight_l)
        part = single(xh_ref[...], w_high) + single(xl_ref[...], w_high) + single(xh_ref[...], w_low)
        part = part.reshape(nv, rows, CHUNK) * weight[None]
        val_ref[0:nv, lanes] = jnp.sum(part, axis=1)

    lane_cap = iota((1, cap), 1)
    for p in range(ndev):
        sent_ref[p, 0:nv, 0:cap] = val_ref[0:nv, p * cap : (p + 1) * cap]
        sent_ref[p, nv : nv + 1, 0:cap] = jnp.where(lane_cap < count_ref[0, p], 1.0, 0.0)

    pl.semaphore_wait(barrier, ndev - 1)

    def fringe(p, q):
        return pltpu.make_async_remote_copy(
            src_ref=sent_ref.at[p], dst_ref=arr_ref.at[q], send_sem=f_send.at[p], recv_sem=f_recv.at[q],
            device_id=(p // ncol, lax.rem(p, ncol)), device_id_type=MESH,
        )

    @pl.loop(1, ndev)
    def _(d):
        fringe(lax.rem(me + d, ndev), me).start()

    arr_ref[me] = sent_ref[me]

    @pl.loop(0, nv)
    def _(v):
        parameters(par_ref, v, step_ref[v], bj, bk, nrow, ncol)
        row = [par_ref[v, n : n + 1, :] for n in range(6)]
        gj[v], wj[v], uj[v] = line_matrices(
            row[0:2], row[2:4], r, bj, bj * nrow,
            lambda t: lax.shift_right_logical(t, shift_k), lambda t: t & (bk - 1), bk,
            lambda z: jnp.broadcast_to(z[:, None, :], (bj, bk, z.shape[1])).reshape(rows, z.shape[1]),
        )
        gk[v], wk[v], uk[v] = line_matrices(
            row[0:2], row[4:6], c, bk, bk * ncol,
            lambda t: t & (bk - 1), lambda t: lax.shift_right_logical(t, shift_k), bj,
            lambda z: jnp.broadcast_to(z[None], (bj, bk, z.shape[1])).reshape(rows, z.shape[1]),
        )
        inv_ref[v] = 1.0 / (par_ref[v, 11:12, 0:1] + step_ref[v] * shape_ref[...])

    @pl.loop(0, slots // CHUNK)
    def _(t):
        start = pl.multiple_of(t * CHUNK, CHUNK)
        cell = cell_ref[:, pl.ds(start, CHUNK)]
        at_lane = jnp.where(iota((bl, CHUNK), 0) == (cell & (bl - 1)), 1.0, 0.0)
        el_ref[pl.ds(start, CHUNK), :] = at_lane.T.astype(BF16)

    @pl.loop(1, ndev)
    def _(d):
        p = lax.rem(me + ndev - d, ndev)
        fringe(p, p).wait_recv()

    for p in range(ndev):
        val_ref[:, p * cap : (p + 1) * cap] = arr_ref[p, :, 0:cap]

    def halos(g):
        vs = pl.ds(g * half_v, half_v)
        return (
            (r < nrow - 1, r > 0, fill_ref.at[vs, pl.ds(rows - bk, bk)], hj_lo.at[vs], (r + 1, c)),
            (r > 0, r < nrow - 1, fill_ref.at[vs, pl.ds(0, bk)], hj_hi.at[vs], (r - 1, c)),
            (c < ncol - 1, c > 0, ks_lo.at[vs], hk_lo.at[vs], (r, c + 1)),
            (c > 0, c < ncol - 1, ks_hi.at[vs], hk_hi.at[vs], (r, c - 1)),
        )

    def halo(g, h):
        _, _, source, target, device = halos(g)[h]
        return pltpu.make_async_remote_copy(
            src_ref=source, dst_ref=target, send_sem=h_send.at[g, h], recv_sem=h_recv.at[g, h],
            device_id=device, device_id_type=MESH,
        )

    at_row = (iota((rows, slots), 0) == lax.shift_right_logical(cell_ref[...], shift_l)) & (
        val_ref[nv : nv + 1, :] > 0.5
    )
    mask = single(jnp.where(at_row, 1.0, 0.0).astype(BF16), el_ref[...]) > 0.5
    for g in (0, 1):
        for n in range(half_v):
            v = g * half_v + n
            high, low = split(jnp.where(at_row, val_ref[v : v + 1, :], 0.0))
            lhs_ref[2 * n * rows : (2 * n + 1) * rows, :] = high
            lhs_ref[(2 * n + 1) * rows : (2 * n + 2) * rows, :] = low
        placed = single(lhs_ref[...], el_ref[...])
        for n in range(half_v):
            v = g * half_v + n
            value = placed[2 * n * rows : (2 * n + 1) * rows] + placed[(2 * n + 1) * rows : (2 * n + 2) * rows]
            filled = jnp.where(mask, value, x_ref[v])
            fill_ref[v] = filled
            planes = filled.reshape(bj, bk, bl)
            ks_lo[v] = planes[:, bk - 1, :]
            ks_hi[v] = planes[:, 0, :]
        for h in range(4):
            pl.when(halos(g)[h][0])(lambda g=g, h=h: halo(g, h).start())

    for h, buffer in enumerate((hj_lo, hj_hi, hk_lo, hk_hi)):

        @pl.when(jnp.logical_not(halos(0)[h][1]))
        def _(buffer=buffer):
            buffer[...] = jnp.zeros_like(buffer)

    lane = iota((rows, bl), 1)
    k_of = iota((rows, bl), 0) & (bk - 1)

    def spread(plane):
        return jnp.broadcast_to(plane[:, None, :], (bj, bk, bl)).reshape(rows, bl)

    for g in (0, 1):
        for h in range(4):
            pl.when(halos(g)[h][1])(lambda g=g, h=h: halo(g, h).wait_recv())

        @pl.loop(g * half_v, (g + 1) * half_v)
        def _(v):
            f = fill_ref[v]
            total = jnp.concatenate([f[bk:], hj_hi[v]], axis=0) + jnp.concatenate([hj_lo[v], f[:-bk]], axis=0)
            total = total + jnp.where(k_of == bk - 1, spread(hk_hi[v]), pltpu.roll(f, rows - 1, 0))
            total = total + jnp.where(k_of == 0, spread(hk_lo[v]), pltpu.roll(f, 1, 0))
            total = total + jnp.where(lane == bl - 1, 0.0, pltpu.roll(f, bl - 1, 1))
            total = total + jnp.where(lane == 0, 0.0, pltpu.roll(f, 1, 1))
            u = step_ref[v] * (spec_ref[...] * (total - 6.0 * f))
            upd_ref[v] = u
            own_j[v] = dot3(wj[v], u)

    def solve_l(ref):
        count = ref.shape[1]
        for g in (0, 1):
            vs = pl.ds(g * half_v, half_v)
            wave = dot_split(ref[vs].reshape(half_v * count, bl), sh_ref[...], sl_ref[...])
            wave = (wave.reshape(half_v, count, bl) * inv_ref[vs]).reshape(half_v * count, bl)
            ref[vs] = dot_split(wave, sh_ref[...], sl_ref[...]).reshape(half_v, count, bl)

    def chain(position, count, place_of, half, own, arrive, send, s_sem, r_sem, alpha, meanwhile):
        def hop(side, v):
            target = place_of(position + (1 if side == 0 else -1))
            return pltpu.make_async_remote_copy(
                src_ref=send.at[side, v], dst_ref=arrive.at[v, pl.ds(side * half, half)],
                send_sem=s_sem.at[side, v], recv_sem=r_sem.at[side, v], device_id=target, device_id_type=MESH,
            )

        has_in = (position > 0, position < count - 1)
        has_out = (position < count - 1, position > 0)

        def pass_on(side):
            @pl.when(jnp.logical_not(has_in[side]))
            def _():
                arrive[:, pl.ds(side * half, half), :] = jnp.zeros((nv, half, bl), F32)

            @pl.loop(0, nv)
            def _(v):
                pl.when(has_in[side])(lambda: hop(side, v).wait_recv())

                @pl.when(has_out[side])
                def _():
                    came = arrive[v, pl.ds(side * half, half), :]
                    factor = jnp.where(
                        iota((half, bl), 0) < half // 2, par_ref[v, alpha : alpha + 1, 0:1], par_ref[v, alpha + 1 : alpha + 2, 0:1]
                    )
                    send[side, v] = own[v, pl.ds(side * half, half), :] + factor * came
                    hop(side, v).start()

        lower = position < count // 2
        upper = jnp.logical_not(lower)
        inner = (position >= count // 4) & (position < count - count // 4)
        pl.when(inner)(meanwhile)
        pl.when(lower)(lambda: pass_on(0))
        pl.when(upper)(lambda: pass_on(1))
        pl.when(jnp.logical_not(inner))(meanwhile)
        pl.when(lower)(lambda: pass_on(1))
        pl.when(upper)(lambda: pass_on(0))

        def finish():
            for side in (0, 1):

                @pl.when(has_out[side])
                def _(side=side):
                    @pl.loop(0, nv)
                    def _(v):
                        hop(side, v).wait_send()

        return finish

    def local_j():
        solve_l(upd_ref)

        @pl.loop(0, nv)
        def _(v):
            upd_ref[v] = dot3(gj[v], upd_ref[v])

    finish_j = chain(r, nrow, lambda p: (p, c), 2 * bk, own_j, in_j, snd_j, j_send, j_recv, 7, local_j)

    for g in (0, 1):
        vs = pl.ds(g * half_v, half_v)
        wave = dot_split(in_j[vs].reshape(half_v * 4 * bk, bl), sh_ref[...], sl_ref[...])
        wave = (wave.reshape(half_v, 4 * bk, bl) * inv_ref[vs]).reshape(half_v * 4 * bk, bl)
        own_j[vs] = dot_split(wave, sh_ref[...], sl_ref[...]).reshape(half_v, 4 * bk, bl)

    @pl.loop(0, nv)
    def _(v):
        y = upd_ref[v] + dot3(uj[v], own_j[v])
        upd_ref[v] = y
        own_k[v] = dot3(wk[v], y)

    def local_k():
        @pl.loop(0, nv)
        def _(v):
            out_ref[v] = dot3(gk[v], upd_ref[v])

    finish_k = chain(c, ncol, lambda p: (r, p), 2 * bj, own_k, in_k, snd_k, k_send, k_recv, 9, local_k)

    @pl.loop(0, nv)
    def _(v):
        out_ref[v] = out_ref[v] + dot3(uk[v], in_k[v])

    finish_j()
    finish_k()
    for g in (0, 1):
        for h in range(4):
            pl.when(halos(g)[h][0])(lambda g=g, h=h: halo(g, h).wait_send())

    @pl.loop(1, ndev)
    def _(d):
        fringe(lax.rem(me + d, ndev), me).wait_send()


def parameters(par_ref, v, step_scalar, bj, bk, nrow, ncol):
    step = jnp.full((1, 128), step_scalar, F32)
    product = 3.5 * step
    diagonal = 1.0 + product
    unit = (diagonal - product) - ((4.0 * step - product) - 0.5 * step)
    s = step / unit
    root = jnp.sqrt(1.0 - 1.0 / s)
    b = 2.0 + 2.0 * root
    a = 4.0 / (s * b)
    kappa = 1.0 / (s * root * unit)

    def angle(x):
        h = 0.5 * jnp.sqrt(x)
        return 2.0 * jnp.log1p(h + h * h / (1.0 + jnp.sqrt(1.0 + h * h)))

    def scale(x, theta, n):
        return kappa / (2.0 * jnp.sqrt(x + 0.25 * x * x) * (1.0 - jnp.exp(-2.0 * (n + 1) * theta)))

    ta, tb = angle(a), angle(b)
    nj, nk = bj * nrow, bk * ncol
    values = [
        ta, tb, scale(a, ta, nj), -scale(b, tb, nj), scale(a, ta, nk), -scale(b, tb, nk), step,
        jnp.exp(-bj * ta), jnp.exp(-bj * tb), jnp.exp(-bk * ta), jnp.exp(-bk * tb), unit,
    ]
    for n, value in enumerate(values):
        par_ref[v, n : n + 1, :] = value


def sine_constants(n):
    k = np.arange(1, n + 1)
    s = np.sqrt(2.0 / (n + 1)) * np.sin(np.pi * ((k[:, None] * k[None, :]) % (2 * (n + 1))) / (n + 1))
    high = s.astype(ml_dtypes.bfloat16)
    low = (s - high.astype(np.float64)).astype(ml_dtypes.bfloat16)
    lam = 4.0 * np.sin(np.pi * k / (2.0 * (n + 1))) ** 2
    return high, low, (lam + 0.25 * lam * lam).astype(np.float32)[None, :]


def local(nrow, ncol, flow_state, spectral, step_size, fringe_count, donor_base, donor_frac, fringe_cell):
    nv, bj, bk, bl = flow_state.shape
    rows = bj * bk
    ndev = nrow * ncol
    slots = donor_base.shape[0]
    high, low, shape = sine_constants(bl)
    vmem = pl.BlockSpec(memory_space=pltpu.VMEM)
    smem = pl.BlockSpec(memory_space=pltpu.SMEM)
    big = pltpu.VMEM((nv, rows, bl), F32)
    dma = pltpu.SemaphoreType.DMA
    out = pl.pallas_call(
        functools.partial(kernel, nrow, ncol, bj, bk),
        out_shape=jax.ShapeDtypeStruct((nv, rows, bl), F32),
        in_specs=[vmem, vmem, smem, smem] + [vmem] * 6,
        out_specs=vmem,
        scratch_shapes=[
            pltpu.VMEM((ndev, 8, 128), F32),
            pltpu.VMEM((ndev, 8, 128), F32),
            pltpu.VMEM((8, slots), F32),
            big,
            big,
            pltpu.VMEM((nv * rows, bl), BF16),
            pltpu.VMEM((nv * rows, bl), BF16),
            pltpu.VMEM((slots, bl), BF16),
            pltpu.VMEM((nv * rows, slots), BF16),
            pltpu.VMEM((nv, 16, 128), F32),
            pltpu.VMEM((nv, 1, bl), F32),
            pltpu.VMEM((nv, bk, bl), F32),
            pltpu.VMEM((nv, bk, bl), F32),
            pltpu.VMEM((nv, bj, bl), F32),
            pltpu.VMEM((nv, bj, bl), F32),
            pltpu.VMEM((nv, bj, bl), F32),
            pltpu.VMEM((nv, bj, bl), F32),
            pltpu.VMEM((nv, rows, rows), F32),
            pltpu.VMEM((nv, 4 * bk, rows), F32),
            pltpu.VMEM((nv, rows, 4 * bk), F32),
            pltpu.VMEM((nv, rows, rows), F32),
            pltpu.VMEM((nv, 4 * bj, rows), F32),
            pltpu.VMEM((nv, rows, 4 * bj), F32),
            pltpu.VMEM((nv, 4 * bk, bl), F32),
            pltpu.VMEM((nv, 4 * bk, bl), F32),
            pltpu.VMEM((2, nv, 2 * bk, bl), F32),
            pltpu.VMEM((nv, 4 * bj, bl), F32),
            pltpu.VMEM((nv, 4 * bj, bl), F32),
            pltpu.VMEM((2, nv, 2 * bj, bl), F32),
            dma((ndev,)),
            dma((ndev,)),
            dma((2, 4)),
            dma((2, 4)),
            dma((2, nv)),
            dma((2, nv)),
            dma((2, nv)),
            dma((2, nv)),
        ],
        compiler_params=pltpu.CompilerParams(
            collective_id=0, has_side_effects=True, vmem_limit_bytes=56 * 1024 * 1024
        ),
    )(
        flow_state.reshape(nv, rows, bl),
        spectral.reshape(rows, bl),
        step_size,
        fringe_count,
        donor_base.reshape(1, slots),
        donor_frac,
        fringe_cell.reshape(1, slots),
        jnp.asarray(shape),
        jnp.asarray(high),
        jnp.asarray(low),
    )
    return out.reshape(nv, bj, bk, bl)


def solution(mesh):
    placed = (
        P(None, "row", "col", None),
        P("row", "col", None),
        P(),
        P(("row", "col"), None),
        P(("row", "col")),
        P(None, ("row", "col")),
        P(("row", "col")),
    )
    return jax.shard_map(
        functools.partial(local, mesh.shape["row"], mesh.shape["col"]),
        mesh=mesh, in_specs=placed, out_specs=P(None, "row", "col", None), check_vma=False,
    )
```

```python
import functools

import jax
import jax.numpy as jnp
import ml_dtypes
import numpy as np
from jax import lax
from jax.experimental import pallas as pl
from jax.experimental.pallas import tpu as pltpu
from jax.sharding import PartitionSpec as P

F32 = jnp.float32
BF16 = jnp.bfloat16
MESH = pl.DeviceIdType.MESH
CHUNK = 256


def split(a):
    high = a.astype(BF16)
    return high, (a - high.astype(F32)).astype(BF16)


def dot_split(a, b_high, b_low):
    a_high, a_low = split(a)
    single = functools.partial(jnp.dot, preferred_element_type=F32)
    return single(a_high, b_high) + single(a_low, b_high) + single(a_high, b_low)


def iota(shape, dim):
    return lax.broadcasted_iota(jnp.int32, shape, dim)


def decay(distance, theta):
    return jnp.exp(-distance * theta)


def dot3(a, b):
    b_high, b_low = split(b)
    return dot_split(a, b_high, b_low)


def line_matrices(theta, scales, position, block, total, local_of, other_of, others, expand):
    rows = block * others
    first = (position * block).astype(F32)
    n1 = float(total + 1)
    i = first + iota((block, rows), 0).astype(F32) + 1.0
    j = first + local_of(iota((block, rows), 1)).astype(F32) + 1.0
    low, high = jnp.minimum(i, j), jnp.maximum(i, j)
    own = jnp.zeros((block, rows), F32)
    for m in (0, 1):
        own = own + scales[m] * decay(high - low, theta[m]) * (1.0 - decay(2.0 * low, theta[m])) * (
            1.0 - decay(2.0 * (n1 - high), theta[m])
        )
    own = jnp.where(other_of(iota((rows, rows), 0)) == other_of(iota((rows, rows), 1)), expand(own), 0.0)

    j = local_of(iota((1, rows), 1)).astype(F32) + 1.0
    parts = []
    for side in (0, 1):
        for m in (0, 1):
            distance = j if side else block + 1.0 - j
            edge = n1 - first - j if side else first + j
            value = decay(distance, theta[m]) * (1.0 - decay(2.0 * edge, theta[m]))
            same = iota((others, rows), 0) == other_of(iota((others, rows), 1))
            parts.append(jnp.where(same, value, 0.0))
    outgoing = jnp.concatenate(parts, axis=0)

    width = 4 * others
    t = iota((block, width), 1)
    side = t >= 2 * others
    mode = jnp.where(side, t - 2 * others, t) >= others
    angle = jnp.where(mode, theta[1][:, :width], theta[0][:, :width])
    i = iota((block, width), 0).astype(F32) + 1.0
    distance = jnp.where(side, block - i, i - 1.0)
    edge = jnp.where(side, first + i, n1 - first - i)
    incoming = decay(distance, angle) * (1.0 - decay(2.0 * edge, angle))
    incoming = incoming * jnp.where(mode, scales[1][:, :width], scales[0][:, :width])
    other = iota((rows, width), 1) & (others - 1)
    incoming = jnp.where(other == other_of(iota((rows, width), 0)), expand(incoming), 0.0)
    return own, outgoing, incoming


def kernel(
    nrow, ncol, bj, bk,
    x_ref, spec_ref, step_ref, count_ref, base_ref, frac_ref, cell_ref, shape_ref, sh_ref, sl_ref,
    out_ref,
    sent_ref, arr_ref, val_ref, fill_ref, upd_ref, xh_ref, xl_ref, el_ref, lhs_ref, par_ref, inv_ref,
    hj_lo, hj_hi, hk_lo, hk_hi, ks_lo, ks_hi,
    gj, wj, uj, gk, wk, uk,
    own_j, in_j, snd_j, own_k, in_k, snd_k,
    f_send, f_recv, h_send, h_recv, j_send, j_recv, k_send, k_recv,
):
    nv, rows, bl = x_ref.shape
    ndev = nrow * ncol
    r, c = lax.axis_index("row"), lax.axis_index("col")
    me = r * ncol + c
    slots = base_ref.shape[1]
    cap = slots // ndev
    shift_k = bk.bit_length() - 1
    shift_l = bl.bit_length() - 1
    half_v = nv // 2
    single = functools.partial(jnp.dot, preferred_element_type=F32)

    barrier = pltpu.get_barrier_semaphore()

    @pl.loop(1, ndev)
    def _(d):
        p = lax.rem(me + d, ndev)
        pl.semaphore_signal(barrier, inc=1, device_id=(p // ncol, lax.rem(p, ncol)), device_id_type=MESH)

    @pl.loop(0, nv)
    def _(v):
        here = pl.ds(pl.multiple_of(v * rows, rows), rows)
        xh_ref[here, :], xl_ref[here, :] = split(x_ref[v])

    @pl.loop(0, slots // CHUNK)
    def _(t):
        lanes = pl.ds(pl.multiple_of(t * CHUNK, CHUNK), CHUNK)
        base = base_ref[:, lanes]
        fj, fk, fl = frac_ref[0:1, lanes], frac_ref[1:2, lanes], frac_ref[2:3, lanes]
        cell_row = lax.shift_right_logical(base, shift_l)
        cell_l = base & (bl - 1)
        row = iota((rows, CHUNK), 0)
        weight = jnp.zeros((rows, CHUNK), F32)
        for a in (0, 1):
            for b in (0, 1):
                w = (fj if a else 1.0 - fj) * (fk if b else 1.0 - fk)
                weight = jnp.where(row == cell_row + (a * bk + b), w, weight)
        lane = iota((bl, CHUNK), 0)
        weight_l = jnp.where(lane == cell_l, 1.0 - fl, jnp.where(lane == cell_l + 1, fl, 0.0))
        w_high, w_low = split(weight_l)
        part = single(xh_ref[...], w_high) + single(xl_ref[...], w_high) + single(xh_ref[...], w_low)
        part = part.reshape(nv, rows, CHUNK) * weight[None]
        val_ref[0:nv, lanes] = jnp.sum(part, axis=1)

    lane_cap = iota((1, cap), 1)
    for p in range(ndev):
        sent_ref[p, 0:nv, 0:cap] = val_ref[0:nv, p * cap : (p + 1) * cap]
        sent_ref[p, nv : nv + 1, 0:cap] = jnp.where(lane_cap < count_ref[0, p], 1.0, 0.0)

    pl.semaphore_wait(barrier, ndev - 1)

    def fringe(p, q):
        return pltpu.make_async_remote_copy(
            src_ref=sent_ref.at[p], dst_ref=arr_ref.at[q], send_sem=f_send.at[p], recv_sem=f_recv.at[q],
            device_id=(p // ncol, lax.rem(p, ncol)), device_id_type=MESH,
        )

    @pl.loop(1, ndev)
    def _(d):
        fringe(lax.rem(me + d, ndev), me).start()

    arr_ref[me] = sent_ref[me]

    @pl.loop(0, nv)
    def _(v):
        parameters(par_ref, v, step_ref[v], bj, bk, nrow, ncol)
        row = [par_ref[v, n : n + 1, :] for n in range(6)]
        gj[v], wj[v], uj[v] = line_matrices(
            row[0:2], row[2:4], r, bj, bj * nrow,
            lambda t: lax.shift_right_logical(t, shift_k), lambda t: t & (bk - 1), bk,
            lambda z: jnp.broadcast_to(z[:, None, :], (bj, bk, z.shape[1])).reshape(rows, z.shape[1]),
        )
        gk[v], wk[v], uk[v] = line_matrices(
            row[0:2], row[4:6], c, bk, bk * ncol,
            lambda t: t & (bk - 1), lambda t: lax.shift_right_logical(t, shift_k), bj,
            lambda z: jnp.broadcast_to(z[None], (bj, bk, z.shape[1])).reshape(rows, z.shape[1]),
        )
        inv_ref[v] = 1.0 / (par_ref[v, 11:12, 0:1] + step_ref[v] * shape_ref[...])

    @pl.loop(0, slots // CHUNK)
    def _(t):
        start = pl.multiple_of(t * CHUNK, CHUNK)
        cell = cell_ref[:, pl.ds(start, CHUNK)]
        at_lane = jnp.where(iota((bl, CHUNK), 0) == (cell & (bl - 1)), 1.0, 0.0)
        el_ref[pl.ds(start, CHUNK), :] = at_lane.T.astype(BF16)

    @pl.loop(1, ndev)
    def _(d):
        p = lax.rem(me + ndev - d, ndev)
        fringe(p, p).wait_recv()

    for p in range(ndev):
        val_ref[:, p * cap : (p + 1) * cap] = arr_ref[p, :, 0:cap]

    def halos(g):
        vs = pl.ds(g * half_v, half_v)
        return (
            (r < nrow - 1, r > 0, fill_ref.at[vs, pl.ds(rows - bk, bk)], hj_lo.at[vs], (r + 1, c)),
            (r > 0, r < nrow - 1, fill_ref.at[vs, pl.ds(0, bk)], hj_hi.at[vs], (r - 1, c)),
            (c < ncol - 1, c > 0, ks_lo.at[vs], hk_lo.at[vs], (r, c + 1)),
            (c > 0, c < ncol - 1, ks_hi.at[vs], hk_hi.at[vs], (r, c - 1)),
        )

    def halo(g, h):
        _, _, source, target, device = halos(g)[h]
        return pltpu.make_async_remote_copy(
            src_ref=source, dst_ref=target, send_sem=h_send.at[g, h], recv_sem=h_recv.at[g, h],
            device_id=device, device_id_type=MESH,
        )

    at_row = (iota((rows, slots), 0) == lax.shift_right_logical(cell_ref[...], shift_l)) & (
        val_ref[nv : nv + 1, :] > 0.5
    )
    mask = single(jnp.where(at_row, 1.0, 0.0).astype(BF16), el_ref[...]) > 0.5
    for g in (0, 1):
        for n in range(half_v):
            v = g * half_v + n
            high, low = split(jnp.where(at_row, val_ref[v : v + 1, :], 0.0))
            lhs_ref[2 * n * rows : (2 * n + 1) * rows, :] = high
            lhs_ref[(2 * n + 1) * rows : (2 * n + 2) * rows, :] = low
        placed = single(lhs_ref[...], el_ref[...])
        for n in range(half_v):
            v = g * half_v + n
            value = placed[2 * n * rows : (2 * n + 1) * rows] + placed[(2 * n + 1) * rows : (2 * n + 2) * rows]
            filled = jnp.where(mask, value, x_ref[v])
            fill_ref[v] = filled
            planes = filled.reshape(bj, bk, bl)
            ks_lo[v] = planes[:, bk - 1, :]
            ks_hi[v] = planes[:, 0, :]
        for h in range(4):
            pl.when(halos(g)[h][0])(lambda g=g, h=h: halo(g, h).start())

    for h, buffer in enumerate((hj_lo, hj_hi, hk_lo, hk_hi)):

        @pl.when(jnp.logical_not(halos(0)[h][1]))
        def _(buffer=buffer):
            buffer[...] = jnp.zeros_like(buffer)

    def solve_l(ref):
        count = ref.shape[1]
        for g in (0, 1):
            vs = pl.ds(g * half_v, half_v)
            wave = dot_split(ref[vs].reshape(half_v * count, bl), sh_ref[...], sl_ref[...])
            wave = (wave.reshape(half_v, count, bl) * inv_ref[vs]).reshape(half_v * count, bl)
            ref[vs] = dot_split(wave, sh_ref[...], sl_ref[...]).reshape(half_v, count, bl)

    def chain(position, count, place_of, half, own, arrive, send, s_sem, r_sem, alpha, meanwhile):
        def hop(side, v):
            target = place_of(position + (1 if side == 0 else -1))
            return pltpu.make_async_remote_copy(
                src_ref=send.at[side, v], dst_ref=arrive.at[v, pl.ds(side * half, half)],
                send_sem=s_sem.at[side, v], recv_sem=r_sem.at[side, v], device_id=target, device_id_type=MESH,
            )

        has_in = (position > 0, position < count - 1)
        has_out = (position < count - 1, position > 0)

        def head(v):
            for side in (0, 1):

                @pl.when(has_out[side] & jnp.logical_not(has_in[side]))
                def _(side=side):
                    send[side, v] = own[v, pl.ds(side * half, half), :]
                    hop(side, v).start()

        def pass_on(side):
            @pl.when(jnp.logical_not(has_in[side]))
            def _():
                arrive[:, pl.ds(side * half, half), :] = jnp.zeros((nv, half, bl), F32)

            @pl.when(has_in[side])
            def _():
                @pl.loop(0, nv)
                def _(v):
                    hop(side, v).wait_recv()

                    @pl.when(has_out[side])
                    def _():
                        came = arrive[v, pl.ds(side * half, half), :]
                        factor = jnp.where(
                            iota((half, bl), 0) < half // 2,
                            par_ref[v, alpha : alpha + 1, 0:1],
                            par_ref[v, alpha + 1 : alpha + 2, 0:1],
                        )
                        send[side, v] = own[v, pl.ds(side * half, half), :] + factor * came
                        hop(side, v).start()

        def run():
            lower = position < count // 2
            upper = jnp.logical_not(lower)
            inner = (position >= count // 4) & (position < count - count // 4)
            pl.when(inner)(meanwhile)
            pl.when(lower)(lambda: pass_on(0))
            pl.when(upper)(lambda: pass_on(1))
            pl.when(jnp.logical_not(inner))(meanwhile)
            pl.when(lower)(lambda: pass_on(1))
            pl.when(upper)(lambda: pass_on(0))

        def finish():
            for side in (0, 1):

                @pl.when(has_out[side])
                def _(side=side):
                    @pl.loop(0, nv)
                    def _(v):
                        hop(side, v).wait_send()

        return head, run, finish

    def local_j():
        solve_l(upd_ref)

        @pl.loop(0, nv)
        def _(v):
            upd_ref[v] = dot3(gj[v], upd_ref[v])

    head_j, run_j, finish_j = chain(r, nrow, lambda p: (p, c), 2 * bk, own_j, in_j, snd_j, j_send, j_recv, 7, local_j)

    lane = iota((rows, bl), 1)
    k_of = iota((rows, bl), 0) & (bk - 1)

    def spread(plane):
        return jnp.broadcast_to(plane[:, None, :], (bj, bk, bl)).reshape(rows, bl)

    for g in (0, 1):
        for h in range(4):
            pl.when(halos(g)[h][1])(lambda g=g, h=h: halo(g, h).wait_recv())

        @pl.loop(g * half_v, (g + 1) * half_v)
        def _(v):
            f = fill_ref[v]
            total = jnp.concatenate([f[bk:], hj_hi[v]], axis=0) + jnp.concatenate([hj_lo[v], f[:-bk]], axis=0)
            total = total + jnp.where(k_of == bk - 1, spread(hk_hi[v]), pltpu.roll(f, rows - 1, 0))
            total = total + jnp.where(k_of == 0, spread(hk_lo[v]), pltpu.roll(f, 1, 0))
            total = total + jnp.where(lane == bl - 1, 0.0, pltpu.roll(f, bl - 1, 1))
            total = total + jnp.where(lane == 0, 0.0, pltpu.roll(f, 1, 1))
            u = step_ref[v] * (spec_ref[...] * (total - 6.0 * f))
            upd_ref[v] = u
            own_j[v] = dot3(wj[v], u)
            head_j(v)

    run_j()

    for g in (0, 1):
        vs = pl.ds(g * half_v, half_v)
        wave = dot_split(in_j[vs].reshape(half_v * 4 * bk, bl), sh_ref[...], sl_ref[...])
        wave = (wave.reshape(half_v, 4 * bk, bl) * inv_ref[vs]).reshape(half_v * 4 * bk, bl)
        own_j[vs] = dot_split(wave, sh_ref[...], sl_ref[...]).reshape(half_v, 4 * bk, bl)

    def local_k():
        @pl.loop(0, nv)
        def _(v):
            out_ref[v] = dot3(gk[v], upd_ref[v])

    head_k, run_k, finish_k = chain(c, ncol, lambda p: (r, p), 2 * bj, own_k, in_k, snd_k, k_send, k_recv, 9, local_k)

    @pl.loop(0, nv)
    def _(v):
        y = upd_ref[v] + dot3(uj[v], own_j[v])
        upd_ref[v] = y
        own_k[v] = dot3(wk[v], y)
        head_k(v)

    run_k()

    @pl.loop(0, nv)
    def _(v):
        out_ref[v] = out_ref[v] + dot3(uk[v], in_k[v])

    finish_j()
    finish_k()
    for g in (0, 1):
        for h in range(4):
            pl.when(halos(g)[h][0])(lambda g=g, h=h: halo(g, h).wait_send())

    @pl.loop(1, ndev)
    def _(d):
        fringe(lax.rem(me + d, ndev), me).wait_send()


def parameters(par_ref, v, step_scalar, bj, bk, nrow, ncol):
    step = jnp.full((1, 128), step_scalar, F32)
    product = 3.5 * step
    diagonal = 1.0 + product
    unit = (diagonal - product) - ((4.0 * step - product) - 0.5 * step)
    s = step / unit
    root = jnp.sqrt(1.0 - 1.0 / s)
    b = 2.0 + 2.0 * root
    a = 4.0 / (s * b)
    kappa = 1.0 / (s * root * unit)

    def angle(x):
        h = 0.5 * jnp.sqrt(x)
        return 2.0 * jnp.log1p(h + h * h / (1.0 + jnp.sqrt(1.0 + h * h)))

    def scale(x, theta, n):
        return kappa / (2.0 * jnp.sqrt(x + 0.25 * x * x) * (1.0 - jnp.exp(-2.0 * (n + 1) * theta)))

    ta, tb = angle(a), angle(b)
    nj, nk = bj * nrow, bk * ncol
    values = [
        ta, tb, scale(a, ta, nj), -scale(b, tb, nj), scale(a, ta, nk), -scale(b, tb, nk), step,
        jnp.exp(-bj * ta), jnp.exp(-bj * tb), jnp.exp(-bk * ta), jnp.exp(-bk * tb), unit,
    ]
    for n, value in enumerate(values):
        par_ref[v, n : n + 1, :] = value


def sine_constants(n):
    k = np.arange(1, n + 1)
    s = np.sqrt(2.0 / (n + 1)) * np.sin(np.pi * ((k[:, None] * k[None, :]) % (2 * (n + 1))) / (n + 1))
    high = s.astype(ml_dtypes.bfloat16)
    low = (s - high.astype(np.float64)).astype(ml_dtypes.bfloat16)
    lam = 4.0 * np.sin(np.pi * k / (2.0 * (n + 1))) ** 2
    return high, low, (lam + 0.25 * lam * lam).astype(np.float32)[None, :]


def local(nrow, ncol, flow_state, spectral, step_size, fringe_count, donor_base, donor_frac, fringe_cell):
    nv, bj, bk, bl = flow_state.shape
    rows = bj * bk
    ndev = nrow * ncol
    slots = donor_base.shape[0]
    high, low, shape = sine_constants(bl)
    vmem = pl.BlockSpec(memory_space=pltpu.VMEM)
    smem = pl.BlockSpec(memory_space=pltpu.SMEM)
    big = pltpu.VMEM((nv, rows, bl), F32)
    dma = pltpu.SemaphoreType.DMA
    out = pl.pallas_call(
        functools.partial(kernel, nrow, ncol, bj, bk),
        out_shape=jax.ShapeDtypeStruct((nv, rows, bl), F32),
        in_specs=[vmem, vmem, smem, smem] + [vmem] * 6,
        out_specs=vmem,
        scratch_shapes=[
            pltpu.VMEM((ndev, 8, 128), F32),
            pltpu.VMEM((ndev, 8, 128), F32),
            pltpu.VMEM((8, slots), F32),
            big,
            big,
            pltpu.VMEM((nv * rows, bl), BF16),
            pltpu.VMEM((nv * rows, bl), BF16),
            pltpu.VMEM((slots, bl), BF16),
            pltpu.VMEM((nv * rows, slots), BF16),
            pltpu.VMEM((nv, 16, 128), F32),
            pltpu.VMEM((nv, 1, bl), F32),
            pltpu.VMEM((nv, bk, bl), F32),
            pltpu.VMEM((nv, bk, bl), F32),
            pltpu.VMEM((nv, bj, bl), F32),
            pltpu.VMEM((nv, bj, bl), F32),
            pltpu.VMEM((nv, bj, bl), F32),
            pltpu.VMEM((nv, bj, bl), F32),
            pltpu.VMEM((nv, rows, rows), F32),
            pltpu.VMEM((nv, 4 * bk, rows), F32),
            pltpu.VMEM((nv, rows, 4 * bk), F32),
            pltpu.VMEM((nv, rows, rows), F32),
            pltpu.VMEM((nv, 4 * bj, rows), F32),
            pltpu.VMEM((nv, rows, 4 * bj), F32),
            pltpu.VMEM((nv, 4 * bk, bl), F32),
            pltpu.VMEM((nv, 4 * bk, bl), F32),
            pltpu.VMEM((2, nv, 2 * bk, bl), F32),
            pltpu.VMEM((nv, 4 * bj, bl), F32),
            pltpu.VMEM((nv, 4 * bj, bl), F32),
            pltpu.VMEM((2, nv, 2 * bj, bl), F32),
            dma((ndev,)),
            dma((ndev,)),
            dma((2, 4)),
            dma((2, 4)),
            dma((2, nv)),
            dma((2, nv)),
            dma((2, nv)),
            dma((2, nv)),
        ],
        compiler_params=pltpu.CompilerParams(
            collective_id=0, has_side_effects=True, vmem_limit_bytes=56 * 1024 * 1024
        ),
    )(
        flow_state.reshape(nv, rows, bl),
        spectral.reshape(rows, bl),
        step_size,
        fringe_count,
        donor_base.reshape(1, slots),
        donor_frac,
        fringe_cell.reshape(1, slots),
        jnp.asarray(shape),
        jnp.asarray(high),
        jnp.asarray(low),
    )
    return out.reshape(nv, bj, bk, bl)


def solution(mesh):
    placed = (
        P(None, "row", "col", None),
        P("row", "col", None),
        P(),
        P(("row", "col"), None),
        P(("row", "col")),
        P(None, ("row", "col")),
        P(("row", "col")),
    )
    return jax.shard_map(
        functools.partial(local, mesh.shape["row"], mesh.shape["col"]),
        mesh=mesh, in_specs=placed, out_specs=P(None, "row", "col", None), check_vma=False,
    )
```
